256 devices in a mesh: runs: 16 (over y, z_lo, core), blocks: 16 (over x, z_hi).
Axes of the slice: x: 4, y: 4, z: 8 (z_hi: 4, z_lo: 2; z = z_hi * 2 + z_lo), core: 2. Of those that a mesh axis runs over, the one named last changes fastest.
Arguments:
- signs: bfloat16 [16384, 49152], P('runs', 'blocks'), may hold values from -1 to 1, as said below
- targets: float32 [16384, 128], P('runs'), may hold values from -6 to 6
- weights: float32 [49152, 128], P('blocks'), may hold values from -6 to 6
Outputs:
- fitted: float32 [49152, 128], P('blocks')
- residual: float32 [16384, 128], P(('runs', 'blocks'))
The draws below stay inside these ranges and needn't reach their ends.
Inputs may be any that keep to these rules, and one draw needn't show every extreme that they name: `signs`: every entry is +1 or -1.
All inputs are finite; a program needn't handle non-finite values.
Results may differ from the reference program's by a relative error of at most 0.004.
Values may be sent and summed in bfloat16 or wider, within the bound.
No kernel may reach another device: no remote copies, remote signals or barrier semaphores. Data moves between devices by JAX's collectives and lax.ppermute only.
A program may use at most 64 MiB of HBM per device.

```python
import math
import jax
import jax.numpy as jnp
from jax import lax

K = 128
ITERS = 3
RUNS = 16384
BLOCKS = 49152


def draw_signs(key, part):
    key = jax.random.fold_in(key, 11)
    coins = jax.random.randint(key, (RUNS, BLOCKS), 0, 2)
    return (coins * 2 - 1).astype(jnp.float32).astype(jnp.bfloat16)


def shard_levels(rng, dims, pieces, smallest, high):
    factor_of, own = 1.0, jax.random.fold_in(rng, 6)
    for position, parts in pieces:
        steps = jnp.exp(jax.random.uniform(jax.random.fold_in(own, position), (parts,), jnp.float32, smallest / len(pieces), high / len(pieces)))
        factor_of = factor_of * jnp.repeat(steps, dims[position] // parts).reshape([-1 if axis == position else 1 for axis in range(len(dims))])
    return factor_of


def centred(stream_key, dims, deviation, bound, split=(), held_as=jnp.bfloat16):
    loudness = shard_levels(stream_key, dims, split, -0.22, 0.18) if split else 1.0
    result = jax.random.normal(stream_key, dims, jnp.float32) * deviation * loudness
    return jnp.minimum(jnp.maximum(result, -bound), bound).astype(held_as)


def setup_inputs(seed: int = 0) -> dict:
    key_of = jax.random.split(jax.random.key(seed), 4)
    return {
        "signs": draw_signs(jax.random.fold_in(key_of[3], 71), 0),
        "targets": centred(key_of[1], (RUNS, K), 1.0, 6.0, ((0, 16),), jnp.float32),
        "weights": centred(key_of[2], (BLOCKS, K), 1.0, 6.0, ((0, 16),), jnp.float32),
    }


def reference(signs, targets, weights):
    total_runs = signs.shape[0]
    total_blocks = signs.shape[1]
    scale_factor = 1.0 / math.sqrt(total_blocks)
    step_size = 1.0 / (1.0 + math.sqrt(total_runs / total_blocks)) ** 2
    limit_value = 0.5 * step_size
    fitted = weights
    residual = targets
    for turn in range(ITERS):
        weight_half = fitted.astype(jnp.bfloat16)
        predicted = scale_factor * jnp.dot(signs, weight_half, preferred_element_type=jnp.float32)
        residual = predicted - targets
        residual_half = residual.astype(jnp.bfloat16)
        gradient = scale_factor * lax.dot_general(signs, residual_half, (((0,), (0,)), ((), ())), preferred_element_type=jnp.float32)
        moved = fitted - step_size * gradient
        fitted = jnp.sign(moved) * jnp.maximum(jnp.abs(moved) - limit_value, 0.0)
    return (fitted, residual)
```

```python
import math

import jax
import jax.numpy as jnp
from jax import lax
from jax.sharding import PartitionSpec as P

ITERS = 3


def shrink(moved, limit_value):
    return jnp.sign(moved) * jnp.maximum(jnp.abs(moved) - limit_value, 0.0)


def sum_share(partial, axis):
    parts = lax.axis_size(axis)
    rows = partial.shape[0] // parts
    pieces = partial.astype(jnp.bfloat16).reshape(parts, rows, partial.shape[1])
    pieces = lax.all_to_all(pieces, axis, 0, 0)
    return jnp.sum(pieces.astype(jnp.float32), axis=0)


def gather_shares(share, axis):
    parts = lax.axis_size(axis)
    pieces = jnp.broadcast_to(share[None], (parts,) + share.shape)
    pieces = lax.all_to_all(pieces, axis, 0, 0)
    return pieces.reshape(parts * share.shape[0], share.shape[1])


def body(signs, targets, weights):
    run_dev = signs.shape[0]
    blk_dev = signs.shape[1]
    runs_count = lax.axis_size("runs")
    blocks_count = lax.axis_size("blocks")
    total_runs = run_dev * runs_count
    total_blocks = blk_dev * blocks_count
    scale_factor = 1.0 / math.sqrt(total_blocks)
    step_size = 1.0 / (1.0 + math.sqrt(total_runs / total_blocks)) ** 2
    limit_value = 0.5 * step_size
    run_share = run_dev // blocks_count
    blk_share = blk_dev // runs_count
    targets_own = lax.dynamic_slice_in_dim(targets, lax.axis_index("blocks") * run_share, run_share, 0)
    fitted_own = lax.dynamic_slice_in_dim(weights, lax.axis_index("runs") * blk_share, blk_share, 0)
    weight_half = weights.astype(jnp.bfloat16)
    for turn in range(ITERS):
        partial_pred = jnp.dot(signs, weight_half, preferred_element_type=jnp.float32)
        residual_own = sum_share(partial_pred, "blocks") * scale_factor - targets_own
        residual_half = gather_shares(residual_own.astype(jnp.bfloat16), "blocks")
        partial_grad = lax.dot_general(
            signs, residual_half, (((0,), (0,)), ((), ())), preferred_element_type=jnp.float32
        )
        gradient_own = sum_share(partial_grad, "runs") * scale_factor
        fitted_own = shrink(fitted_own - step_size * gradient_own, limit_value)
        weight_half = gather_shares(fitted_own.astype(jnp.bfloat16), "runs")
    return (weight_half.astype(jnp.float32), residual_own)


def solution(mesh):
    in_specs = (P("runs", "blocks"), P("runs", None), P("blocks", None))
    out_specs = (P("blocks", None), P(("runs", "blocks"), None))
    return jax.shard_map(body, mesh=mesh, in_specs=in_specs, out_specs=out_specs, check_vma=False)
```

```python
import functools
import math

import jax
import jax.numpy as jnp
from jax import lax
from jax.experimental import pallas as pl
from jax.experimental.pallas import tpu as pltpu
from jax.sharding import PartitionSpec as P

ITERS = 3
BF = jnp.bfloat16
F32 = jnp.float32

X_UNIT, ZHI_UNIT = 4, 1
Y_UNIT, ZLO_UNIT, CORE_UNIT = 4, 2, 1
AT_X, AT_ZHI, AT_Y, AT_CORE = range(4)

VMEM_LIMIT = 16 << 20


def shrink(moved, limit_value):
    size = jnp.maximum(jnp.abs(moved) - limit_value, 0.0)
    return jnp.where(moved < 0.0, -size, size)


def swap(array, axis, flip):
    return lax.ppermute(array, axis, [(i, i ^ flip) for i in range(lax.axis_size(axis))])


def swap4(pieces, axis, unit, order):
    got = {s: swap(pieces[s], axis, s * unit) for s in order}
    return [got[s] for s in (1, 2, 3)]


def call(kernel, name, place, args, outs, scratch=(), flops=0):
    vmem = pl.BlockSpec(memory_space=pltpu.VMEM)
    moved = sum(math.prod(a.shape) * a.dtype.itemsize for a in [*args, *outs])
    return pl.pallas_call(
        kernel,
        in_specs=[pl.BlockSpec(memory_space=pltpu.SMEM)] + [vmem] * len(args),
        out_specs=[vmem] * len(outs),
        out_shape=list(outs),
        scratch_shapes=list(scratch),
        compiler_params=pltpu.CompilerParams(vmem_limit_bytes=VMEM_LIMIT),
        cost_estimate=pl.CostEstimate(flops=flops, bytes_accessed=moved, transcendentals=0),
        name=name,
    )(place, *args)


def shape(dims, dtype):
    return jax.ShapeDtypeStruct(dims, dtype)


def part(index, size):
    return pl.ds(pl.multiple_of(index * size, size), size)


def first_kernel(place, s_ref, w_ref, p0, p1, p2, p3, own_ref, held):
    rows, width = p0.shape[0], own_ref.shape[1]
    held[...] = w_ref[...].astype(BF)
    for s, out in enumerate((p0, p1, p2, p3)):
        out[...] = jnp.dot(
            s_ref[part(place[AT_X] ^ s, rows), :], held[...], preferred_element_type=F32
        ).astype(out.dtype)
    own_ref[...] = w_ref[part(place[AT_CORE] * 4 + place[AT_Y], width), :].T


def predict_kernel(place, s_ref, *refs):
    weights, outs, held = refs[:8], refs[8:12], refs[12]
    rows, width = outs[0].shape[0], weights[0].shape[1]
    for core in range(2):
        for s in range(4):
            at = (place[AT_CORE] ^ core) * 4 + (place[AT_Y] ^ s)
            held[:, part(at, width)] = weights[core * 4 + s][...]
    for s, out in enumerate(outs):
        out[...] = lax.dot_general(
            s_ref[part(place[AT_X] ^ s, rows), :], held[...], (((1,), (1,)), ((), ())), preferred_element_type=F32
        ).astype(out.dtype)


def sum_kernel(place, p0, g1, g2, g3, sum_ref, half_ref):
    total = (p0[...] + g1[...].astype(F32)) + (g2[...].astype(F32) + g3[...].astype(F32))
    sum_ref[...] = total
    half_ref[...] = total.astype(BF)


def residual_kernel(scale, place, q_ref, z1, z2, z3, t_ref, half_ref, own_ref):
    rows, share = q_ref.shape[0], own_ref.shape[0]
    total = (q_ref[...] + z1[...].astype(F32)) + (z2[...].astype(F32) + z3[...].astype(F32))
    residual = total * scale - t_ref[part(place[AT_X], rows), :]
    half_ref[...] = residual.T.astype(BF)
    mine = part(place[AT_ZHI], share)
    own = (q_ref[mine, :] + z1[mine, :].astype(F32)) + (z2[mine, :].astype(F32) + z3[mine, :].astype(F32))
    own_ref[...] = own * scale - t_ref[part(place[AT_X] * (rows // share) + place[AT_ZHI], share), :]


def gradient_kernel(other, place, s_ref, r0, r1, r2, r3, out_ref, held):
    rows, half = r0.shape[1], out_ref.shape[1]
    for s, piece in enumerate((r0, r1, r2, r3)):
        held[:, part(place[AT_X] ^ s, rows)] = piece[...]
    columns = part(place[AT_CORE] ^ other, half)
    out_ref[...] = jnp.dot(held[...], s_ref[:, columns], preferred_element_type=F32).astype(out_ref.dtype)


def join_kernel(place, kept, got, p0, p1, p2, p3):
    width = p0.shape[1]
    for s, out in enumerate((p0, p1, p2, p3)):
        at = part(place[AT_Y] ^ s, width)
        out[...] = (kept[:, at] + got[:, at].astype(F32)).astype(out.dtype)


def half_kernel(place, p0, g1, g2, g3, half_ref):
    total = (p0[...] + g1[...].astype(F32)) + (g2[...].astype(F32) + g3[...].astype(F32))
    half_ref[...] = total.astype(BF)


def update_kernel(factor, limit_value, place, kept, got, fitted_ref, new_ref, half_ref):
    gradient = kept[...].astype(F32) + got[...].astype(F32)
    fitted = shrink(fitted_ref[...] - factor * gradient, limit_value)
    new_ref[...] = fitted
    half_ref[...] = fitted.astype(BF)


def place_kernel(place, *refs):
    parts, out_ref = refs[:8], refs[8]
    width = parts[0].shape[1]
    for core in range(2):
        for s in range(4):
            at = (place[AT_CORE] ^ core) * 4 + (place[AT_Y] ^ s)
            out_ref[part(at, width), :] = parts[core * 4 + s][...].astype(F32).T


def body(signs, targets, weights):
    run_dev, blk_dev = signs.shape
    k = weights.shape[1]
    total_runs = run_dev * lax.axis_size("runs")
    total_blocks = blk_dev * lax.axis_size("blocks")
    scale_factor = 1.0 / math.sqrt(total_blocks)
    step_size = 1.0 / (1.0 + math.sqrt(total_runs / total_blocks)) ** 2
    limit_value = 0.5 * step_size
    rows, width, share = run_dev // 4, blk_dev // 8, run_dev // lax.axis_size("blocks")
    at_run, at_block = lax.axis_index("runs"), lax.axis_index("blocks")
    place = jnp.stack([at_block >> 2, at_block & 3, at_run >> 2, at_run & 1]).astype(jnp.int32)
    flops = 2 * run_dev * blk_dev * k
    pred_outs = [shape((rows, k), F32)] + [shape((rows, k), BF)] * 3
    for turn in range(ITERS):
        if turn == 0:
            *pieces, fitted_own = call(
                first_kernel, "first", place, [signs, weights],
                [*pred_outs, shape((k, width), F32)], [pltpu.VMEM((blk_dev, k), BF)], flops,
            )
        else:
            pieces = call(
                predict_kernel, "predict", place, [signs, *weight_parts],
                pred_outs, [pltpu.VMEM((k, blk_dev), BF)], flops,
            )
        got = swap4(pieces, "blocks", X_UNIT, (2, 1, 3))
        summed, half = call(
            sum_kernel, "sum", place, [pieces[0], *got], [shape((rows, k), F32), shape((rows, k), BF)]
        )
        got = swap4([half] * 4, "blocks", ZHI_UNIT, (1, 3, 2))
        half, residual_own = call(
            functools.partial(residual_kernel, scale_factor), "residual", place, [summed, *got, targets],
            [shape((k, rows), BF), shape((share, k), F32)],
        )
        halves = [half] + swap4([half] * 4, "blocks", X_UNIT, (1, 3, 2))
        held = [pltpu.VMEM((k, run_dev), BF)]
        (sent,) = call(
            functools.partial(gradient_kernel, 1), "gradient_sent", place, [signs, *halves],
            [shape((k, blk_dev // 2), BF)], held, flops // 2,
        )
        got = swap(sent, "runs", CORE_UNIT)
        (kept,) = call(
            functools.partial(gradient_kernel, 0), "gradient_kept", place, [signs, *halves],
            [shape((k, blk_dev // 2), F32)], held, flops // 2,
        )
        pieces = call(
            join_kernel, "join", place, [kept, got], [shape((k, width), F32)] + [shape((k, width), BF)] * 3
        )
        got = swap4(pieces, "runs", Y_UNIT, (2, 1, 3))
        (half,) = call(half_kernel, "half", place, [pieces[0], *got], [shape((k, width), BF)])
        got = swap(half, "runs", ZLO_UNIT)
        fitted_own, half = call(
            functools.partial(update_kernel, step_size * scale_factor, limit_value), "update", place,
            [half, got, fitted_own], [shape((k, width), F32), shape((k, width), BF)],
        )
        weight_parts = [half] + swap4([half] * 4, "runs", Y_UNIT, (1, 3, 2))
        weight_parts += [swap(piece, "runs", CORE_UNIT) for piece in weight_parts]
    (fitted,) = call(place_kernel, "place", place, weight_parts, [shape((blk_dev, k), F32)])
    return (fitted, residual_own)


def solution(mesh):
    in_specs = (P("runs", "blocks"), P("runs", None), P("blocks", None))
    out_specs = (P("blocks", None), P(("runs", "blocks"), None))
    return jax.shard_map(body, mesh=mesh, in_specs=in_specs, out_specs=out_specs, check_vma=False)
```

```python
import functools
import math

import jax
import jax.numpy as jnp
from jax import lax
from jax.experimental import pallas as pl
from jax.experimental.pallas import tpu as pltpu
from jax.sharding import PartitionSpec as P

ITERS = 3
BF = jnp.bfloat16
F32 = jnp.float32

X_UNIT, ZHI_UNIT = 4, 1
Y_UNIT, ZLO_UNIT, CORE_UNIT = 4, 2, 1
AT_X, AT_ZHI, AT_Y, AT_CORE = range(4)

VMEM_LIMIT = 16 << 20


def shrink(moved, limit_value):
    size = jnp.maximum(jnp.abs(moved) - limit_value, 0.0)
    return jnp.where(moved < 0.0, -size, size)


def swap(array, axis, flip):
    return lax.ppermute(array, axis, [(i, i ^ flip) for i in range(lax.axis_size(axis))])


def swap4(pieces, axis, unit):
    return [swap(pieces[s], axis, s * unit) for s in (1, 2, 3)]


def call(kernel, name, place, args, outs, scratch=(), flops=0, in_hbm=(), outs_in_hbm=False, aliases=None):
    vmem, hbm = (pl.BlockSpec(memory_space=m) for m in (pltpu.VMEM, pltpu.HBM))
    moved = sum(math.prod(a.shape) * a.dtype.itemsize for a in [*args, *outs])
    return pl.pallas_call(
        kernel,
        in_specs=[pl.BlockSpec(memory_space=pltpu.SMEM)] + [hbm if i in in_hbm else vmem for i in range(len(args))],
        out_specs=[hbm if outs_in_hbm else vmem] * len(outs),
        out_shape=list(outs),
        scratch_shapes=list(scratch),
        input_output_aliases=aliases or {},
        compiler_params=pltpu.CompilerParams(vmem_limit_bytes=VMEM_LIMIT),
        cost_estimate=pl.CostEstimate(flops=flops, bytes_accessed=moved, transcendentals=0),
        name=name,
    )(place, *args)


def shape(dims, dtype):
    return jax.ShapeDtypeStruct(dims, dtype)


def part(index, size):
    return pl.ds(pl.multiple_of(index * size, size), size)


def cut(place, chunk_of, acc, outs):
    rows = outs[0].shape[0]

    @pl.loop(0, 4)
    def _(s):
        acc[s] = chunk_of(part(place[AT_X] ^ s, rows))

    for s, out in enumerate(outs):
        out[...] = acc[s].astype(out.dtype)


def first_kernel(place, s_ref, w_ref, p0, p1, p2, p3, own_ref, held, acc):
    width = own_ref.shape[1]
    held[...] = w_ref[...].astype(BF)
    cut(
        place, lambda at: jnp.dot(s_ref[at, :], held[...], preferred_element_type=F32), acc, (p0, p1, p2, p3)
    )
    own_ref[...] = w_ref[part(place[AT_CORE] * 4 + place[AT_Y], width), :].T


ACROSS = (((1,), (1,)), ((), ()))


def pair_kernel(place, a_ref, b_ref, out_ref):
    width = a_ref.shape[1]
    out_ref[:, :width] = a_ref[...]
    out_ref[:, width:] = b_ref[...]


def put_together(place, pieces, held):
    width = held.shape[1] // 4
    for s, piece in enumerate(pieces):
        held[:, part(place[AT_Y] ^ s, width)] = piece


def own_half_kernel(place, s_ref, w0, w1, w2, w3, acc_ref, held):
    put_together(place, (w0[...], w1[...], w2[...], w3[...]), held)
    columns = part(place[AT_CORE], held.shape[1])
    rows = acc_ref.shape[0] // 4

    @pl.loop(0, 4)
    def _(i):
        at = part(i, rows)
        acc_ref[at, :] = lax.dot_general(s_ref[at, columns], held[...], ACROSS, preferred_element_type=F32)


def other_half_kernel(place, s_ref, acc_ref, w03, w12, p0, p1, p2, p3, held, acc):
    width = held.shape[1] // 4
    put_together(place, (w03[:, :width], w12[:, :width], w12[:, width:], w03[:, width:]), held)
    columns = part(place[AT_CORE] ^ 1, held.shape[1])

    def chunk_of(at):
        rest = lax.dot_general(s_ref[at, columns], held[...], ACROSS, preferred_element_type=F32)
        return acc_ref[at, :] + rest

    cut(place, chunk_of, acc, (p0, p1, p2, p3))


def sum_kernel(place, p0, g1, g2, g3, sum_ref, half_ref):
    total = (p0[...] + g1[...].astype(F32)) + (g2[...].astype(F32) + g3[...].astype(F32))
    sum_ref[...] = total
    half_ref[...] = total.astype(BF)


def sum2_kernel(place, a_ref, b_ref, sum_ref, half_ref):
    total = a_ref[...] + b_ref[...].astype(F32)
    sum_ref[...] = total
    half_ref[...] = total.astype(BF)


def residual_kernel(scale, place, a_ref, b_ref, t_ref, half_ref, *own):
    rows = a_ref.shape[0]
    total = a_ref[...] + b_ref[...].astype(F32)
    residual = total * scale - t_ref[part(place[AT_X], rows), :]
    half_ref[...] = residual.T.astype(BF)
    if own:
        own_ref, held = own
        held[...] = residual
        own_ref[...] = held[part(place[AT_ZHI], own_ref.shape[0]), :]


def gradient_kernel(other, place, s_ref, r0, r1, r2, r3, out_ref, held):
    rows, half = r0.shape[1], out_ref.shape[1]
    for s, piece in enumerate((r0, r1, r2, r3)):
        held[:, part(place[AT_X] ^ s, rows)] = piece[...]
    tile = half // 3

    @pl.loop(0, 3)
    def _(i):
        columns = part((place[AT_CORE] ^ other) * 3 + i, tile)
        out_ref[:, part(i, tile)] = jnp.dot(held[...], s_ref[:, columns], preferred_element_type=F32).astype(out_ref.dtype)


def join_kernel(place, kept, got, p0, p1, p2, p3):
    width = p0.shape[1]
    for s, out in enumerate((p0, p1, p2, p3)):
        at = part(place[AT_Y] ^ s, width)
        out[...] = (kept[:, at] + got[:, at].astype(F32)).astype(out.dtype)


def half_kernel(place, p0, g1, g2, g3, half_ref):
    total = (p0[...] + g1[...].astype(F32)) + (g2[...].astype(F32) + g3[...].astype(F32))
    half_ref[...] = total.astype(BF)


def update_kernel(factor, limit_value, place, kept, got, fitted_ref, new_ref, half_ref):
    gradient = kept[...].astype(F32) + got[...].astype(F32)
    fitted = shrink(fitted_ref[...] - factor * gradient, limit_value)
    new_ref[...] = fitted
    half_ref[...] = fitted.astype(BF)


def place_kernel(other, place, *refs):
    out_hbm, held, sems = refs[-3:]
    width = held.shape[1]
    if other:
        w03, w12 = refs[:2]
        pieces = (w03[:, :width], w12[:, :width], w12[:, width:], w03[:, width:])
    else:
        pieces = [ref[...] for ref in refs[:4]]
    copies = []
    for s, piece in enumerate(pieces):
        held[s] = piece.astype(F32).T
        rows = part((place[AT_CORE] ^ other) * 4 + (place[AT_Y] ^ s), width)
        copies.append(pltpu.make_async_copy(held.at[s], out_hbm.at[rows, :], sems.at[s]))
        copies[-1].start()
    for copy in copies:
        copy.wait()


def body(signs, targets, weights):
    run_dev, blk_dev = signs.shape
    k = weights.shape[1]
    total_runs = run_dev * lax.axis_size("runs")
    total_blocks = blk_dev * lax.axis_size("blocks")
    scale_factor = 1.0 / math.sqrt(total_blocks)
    step_size = 1.0 / (1.0 + math.sqrt(total_runs / total_blocks)) ** 2
    limit_value = 0.5 * step_size
    rows, width, share = run_dev // 4, blk_dev // 8, run_dev // lax.axis_size("blocks")
    at_run, at_block = lax.axis_index("runs"), lax.axis_index("blocks")
    place = jnp.stack([at_block >> 2, at_block & 3, at_run >> 2, at_run & 1]).astype(jnp.int32)
    flops = 2 * run_dev * blk_dev * k
    chunk, chunk_half = shape((rows, k), F32), shape((rows, k), BF)
    piece, piece_half = shape((k, width), F32), shape((k, width), BF)
    cuts = [chunk] + [chunk_half] * 3
    acc_held, w_held = pltpu.VMEM((4, rows, k), F32), pltpu.VMEM((k, blk_dev // 2), BF)
    for turn in range(ITERS):
        if turn == 0:
            *pieces, fitted_own = call(
                first_kernel, "first", place, [signs, weights], [*cuts, piece],
                [pltpu.VMEM((blk_dev, k), BF), acc_held], flops,
            )
        else:
            (acc,) = call(
                own_half_kernel, "own_half", place, [signs, *near], [shape((run_dev, k), F32)], [w_held], flops // 2
            )
            pieces = call(
                other_half_kernel, "other_half", place, [signs, acc, *far], cuts, [w_held, acc_held], flops // 2
            )
        got = swap4(pieces, "blocks", X_UNIT)
        summed, half = call(sum_kernel, "sum", place, [pieces[0], *got], [chunk, chunk_half])
        got = swap(half, "blocks", 1 * ZHI_UNIT)
        summed, half = call(sum2_kernel, "sum2", place, [summed, got], [chunk, chunk_half])
        got = swap(half, "blocks", 3 * ZHI_UNIT)
        last = turn == ITERS - 1
        half, *residual_own = call(
            functools.partial(residual_kernel, scale_factor), "residual", place, [summed, got, targets],
            [shape((k, rows), BF)] + [shape((share, k), F32)] * last, [pltpu.VMEM((rows, k), F32)] * last,
        )
        halves = [half] + swap4([half] * 4, "blocks", X_UNIT)
        held = [pltpu.VMEM((k, run_dev), BF)]
        (sent,) = call(
            functools.partial(gradient_kernel, 1), "gradient_sent", place, [signs, *halves],
            [shape((k, blk_dev // 2), BF)], held, flops // 2,
        )
        got = swap(sent, "runs", CORE_UNIT)
        (kept,) = call(
            functools.partial(gradient_kernel, 0), "gradient_kept", place, [signs, *halves],
            [shape((k, blk_dev // 2), F32)], held, flops // 2,
        )
        pieces = call(join_kernel, "join", place, [kept, got], [piece] + [piece_half] * 3)
        got = swap4(pieces, "runs", Y_UNIT)
        (half,) = call(half_kernel, "half", place, [pieces[0], *got], [piece_half])
        got = swap(half, "runs", ZLO_UNIT)
        fitted_own, half = call(
            functools.partial(update_kernel, step_size * scale_factor, limit_value), "update", place,
            [half, got, fitted_own], [piece, piece_half],
        )
        near = [half] + swap4([half] * 4, "runs", Y_UNIT)
        pairs = [call(pair_kernel, "pair", place, two, [shape((k, 2 * width), BF)])[0] for two in (near[::3], near[1:3])]
        far = [swap(pair, "runs", CORE_UNIT) for pair in pairs]
    held = [pltpu.VMEM((4, width, k), F32), pltpu.SemaphoreType.DMA((4,))]
    whole = [shape((blk_dev, k), F32)]
    fitted = call(functools.partial(place_kernel, 0), "place_near", place, near, whole, held, outs_in_hbm=True)
    (fitted,) = call(
        functools.partial(place_kernel, 1), "place_far", place, [*far, *fitted], whole, held,
        in_hbm=(2,), outs_in_hbm=True, aliases={3: 0},
    )
    return (fitted, residual_own[0])


def solution(mesh):
    in_specs = (P("runs", "blocks"), P("runs", None), P("blocks", None))
    out_specs = (P("blocks", None), P(("runs", "blocks"), None))
    return jax.shard_map(body, mesh=mesh, in_specs=in_specs, out_specs=out_specs, check_vma=False)
```

```python
import functools
import math

import jax
import jax.numpy as jnp
from jax import lax
from jax.experimental import pallas as pl
from jax.experimental.pallas import tpu as pltpu
from jax.sharding import PartitionSpec as P

ITERS = 3
BF = jnp.bfloat16
F32 = jnp.float32

X_UNIT, ZHI_UNIT = 4, 1
Y_UNIT, ZLO_UNIT, CORE_UNIT = 4, 2, 1
AT_X, AT_ZHI, AT_Y, AT_CORE = range(4)

VMEM_LIMIT = 16 << 20


def shrink(moved, limit_value):
    size = jnp.maximum(jnp.abs(moved) - limit_value, 0.0)
    return jnp.where(moved < 0.0, -size, size)


def swap(array, axis, flip):
    return lax.ppermute(array, axis, [(i, i ^ flip) for i in range(lax.axis_size(axis))])


def swap4(pieces, axis, unit):
    return [swap(pieces[s], axis, s * unit) for s in (1, 2, 3)]


def call(kernel, name, place, args, outs, scratch=(), flops=0, in_hbm=(), in_vmem=(), outs_in_hbm=False, aliases=None):
    vmem, hbm = (pl.BlockSpec(memory_space=m) for m in (pltpu.VMEM, pltpu.HBM))
    moved = sum(math.prod(a.shape) * a.dtype.itemsize for a in [*args, *outs])
    args = list(args)
    for i in in_hbm:
        args[i] = pltpu.with_memory_space_constraint(args[i], pltpu.HBM)
    for i in in_vmem:
        args[i] = pltpu.with_memory_space_constraint(args[i], pltpu.VMEM)
    return pl.pallas_call(
        kernel,
        in_specs=[pl.BlockSpec(memory_space=pltpu.SMEM)] + [hbm if i in in_hbm else vmem for i in range(len(args))],
        out_specs=[hbm if outs_in_hbm else vmem] * len(outs),
        out_shape=list(outs),
        scratch_shapes=list(scratch),
        input_output_aliases=aliases or {},
        compiler_params=pltpu.CompilerParams(vmem_limit_bytes=VMEM_LIMIT),
        cost_estimate=pl.CostEstimate(flops=flops, bytes_accessed=moved, transcendentals=0),
        name=name,
    )(place, *args)


def shape(dims, dtype):
    return jax.ShapeDtypeStruct(dims, dtype)


def part(index, size):
    return pl.ds(pl.multiple_of(index * size, size), size)


def cut(place, acc, outs):
    for s, out in enumerate(outs):
        out[...] = acc[part(place[AT_X] ^ s, out.shape[0]), :].astype(out.dtype)


def first_kernel(place, s_hbm, w_hbm, p0, p1, p2, p3, own_ref, s_ref, w_held, half, sems):
    rows, width = p0.shape[0], own_ref.shape[1]
    load_w = pltpu.make_async_copy(w_hbm, w_held, sems.at[4])
    load_w.start()
    loads = []
    for s in range(4):
        at = part(place[AT_X] ^ s, rows)
        loads.append(pltpu.make_async_copy(s_hbm.at[at, :], s_ref.at[at, :], sems.at[s]))
        loads[s].start()
    load_w.wait()
    half[...] = w_held[...].astype(BF)
    own_ref[...] = w_held[part(place[AT_CORE] * 4 + place[AT_Y], width), :].T
    for s, out in enumerate((p0, p1, p2, p3)):
        loads[s].wait()
        at = part(place[AT_X] ^ s, rows)
        out[...] = jnp.dot(s_ref[at, :], half[...], preferred_element_type=F32).astype(out.dtype)


def load_kernel(place, s_hbm, after, s_ref, sems):
    rows = s_ref.shape[0] // 4
    loads = [pltpu.make_async_copy(s_hbm.at[part(i, rows), :], s_ref.at[part(i, rows), :], sems.at[i]) for i in range(4)]
    for load in loads:
        load.start()
    for load in loads:
        load.wait()


def half_product(place, other, s_ref, pieces, held):
    half = held.shape[1]
    for s, piece in enumerate(pieces):
        held[:, part(place[AT_Y] ^ s, half // 4)] = piece[...]
    columns = part(place[AT_CORE] ^ other, half)
    return lax.dot_general(s_ref[:, columns], held[...], (((1,), (1,)), ((), ())), preferred_element_type=F32)


def own_half_kernel(place, s_ref, w0, w1, w2, w3, acc_ref, held):
    acc_ref[...] = half_product(place, 0, s_ref, (w0, w1, w2, w3), held)


def other_half_kernel(place, s_ref, acc_ref, w0, w1, w2, w3, p0, p1, p2, p3, held, acc):
    acc[...] = acc_ref[...] + half_product(place, 1, s_ref, (w0, w1, w2, w3), held)
    cut(place, acc, (p0, p1, p2, p3))


def sum_kernel(place, p0, g1, g2, g3, sum_ref, half_ref):
    total = (p0[...] + g1[...].astype(F32)) + (g2[...].astype(F32) + g3[...].astype(F32))
    sum_ref[...] = total
    half_ref[...] = total.astype(BF)


def residual_kernel(scale, place, q_ref, z1, z2, z3, t_ref, half_ref, *own):
    rows = q_ref.shape[0]
    total = (q_ref[...] + z1[...].astype(F32)) + (z2[...].astype(F32) + z3[...].astype(F32))
    residual = total * scale - t_ref[part(place[AT_X], rows), :]
    half_ref[...] = residual.T.astype(BF)
    if own:
        own_ref, held = own
        held[...] = residual
        own_ref[...] = held[part(place[AT_ZHI], own_ref.shape[0]), :]


def gradient_kernel(other, place, s_ref, r0, r1, r2, r3, out_ref, held):
    rows, half = r0.shape[1], out_ref.shape[1]
    for s, piece in enumerate((r0, r1, r2, r3)):
        held[:, part(place[AT_X] ^ s, rows)] = piece[...]
    columns = part(place[AT_CORE] ^ other, half)
    out_ref[...] = jnp.dot(held[...], s_ref[:, columns], preferred_element_type=F32).astype(out_ref.dtype)


def join_kernel(place, kept, got, p0, p1, p2, p3):
    width = p0.shape[1]
    for s, out in enumerate((p0, p1, p2, p3)):
        at = part(place[AT_Y] ^ s, width)
        out[...] = (kept[:, at] + got[:, at].astype(F32)).astype(out.dtype)


def half_kernel(place, p0, g1, g2, g3, half_ref):
    total = (p0[...] + g1[...].astype(F32)) + (g2[...].astype(F32) + g3[...].astype(F32))
    half_ref[...] = total.astype(BF)


def update_kernel(factor, limit_value, place, kept, got, fitted_ref, new_ref, half_ref):
    gradient = kept[...].astype(F32) + got[...].astype(F32)
    fitted = shrink(fitted_ref[...] - factor * gradient, limit_value)
    new_ref[...] = fitted
    half_ref[...] = fitted.astype(BF)


def place_kernel(other, place, *refs):
    out_hbm, held, sems = refs[-3:]
    width = held.shape[1]
    copies = []
    for s, piece in enumerate(refs[:4]):
        held[s] = piece[...].astype(F32).T
        rows = part((place[AT_CORE] ^ other) * 4 + (place[AT_Y] ^ s), width)
        copies.append(pltpu.make_async_copy(held.at[s], out_hbm.at[rows, :], sems.at[s]))
        copies[-1].start()
    for copy in copies:
        copy.wait()


def body(signs, targets, weights):
    run_dev, blk_dev = signs.shape
    k = weights.shape[1]
    total_runs = run_dev * lax.axis_size("runs")
    total_blocks = blk_dev * lax.axis_size("blocks")
    scale_factor = 1.0 / math.sqrt(total_blocks)
    step_size = 1.0 / (1.0 + math.sqrt(total_runs / total_blocks)) ** 2
    limit_value = 0.5 * step_size
    rows, width, share = run_dev // 4, blk_dev // 8, run_dev // lax.axis_size("blocks")
    at_run, at_block = lax.axis_index("runs"), lax.axis_index("blocks")
    place = jnp.stack([at_block >> 2, at_block & 3, at_run >> 2, at_run & 1]).astype(jnp.int32)
    flops = 2 * run_dev * blk_dev * k
    chunk, chunk_half = shape((rows, k), F32), shape((rows, k), BF)
    piece, piece_half = shape((k, width), F32), shape((k, width), BF)
    cuts = [chunk] + [chunk_half] * 3
    acc, acc_held, w_held = shape((run_dev, k), F32), pltpu.VMEM((run_dev, k), F32), pltpu.VMEM((k, blk_dev // 2), BF)

    def load(after):
        (loaded,) = call(
            load_kernel, "load", place, [signs, after], [pltpu.VMEM(signs.shape, BF)],
            [pltpu.SemaphoreType.DMA((4,))], in_hbm=(0,),
        )
        return loaded

    def step(pieces, fitted_own, last):
        got = swap4(pieces, "blocks", X_UNIT)
        summed, half = call(sum_kernel, "sum", place, [pieces[0], *got], [chunk, chunk_half])
        got = swap4([half] * 4, "blocks", ZHI_UNIT)
        loaded = load(half)
        half, *residual_own = call(
            functools.partial(residual_kernel, scale_factor), "residual", place, [summed, *got, targets],
            [shape((k, rows), BF)] + [shape((share, k), F32)] * last, [pltpu.VMEM((rows, k), F32)] * last,
        )
        halves = [half] + swap4([half] * 4, "blocks", X_UNIT)
        held = [pltpu.VMEM((k, run_dev), BF)]
        (sent,) = call(
            functools.partial(gradient_kernel, 1), "gradient_sent", place, [loaded, *halves],
            [shape((k, blk_dev // 2), BF)], held, flops // 2, in_vmem=(0,),
        )
        got = swap(sent, "runs", CORE_UNIT)
        (kept,) = call(
            functools.partial(gradient_kernel, 0), "gradient_kept", place, [loaded, *halves],
            [shape((k, blk_dev // 2), F32)], held, flops // 2, in_vmem=(0,),
        )
        pieces = call(join_kernel, "join", place, [kept, got], [piece] + [piece_half] * 3)
        got = swap4(pieces, "runs", Y_UNIT)
        (half,) = call(half_kernel, "half", place, [pieces[0], *got], [piece_half])
        got = swap(half, "runs", ZLO_UNIT)
        fitted_own, half = call(
            functools.partial(update_kernel, step_size * scale_factor, limit_value), "update", place,
            [half, got, fitted_own], [piece, piece_half], aliases={3: 0},
        )
        near = [half] + swap4([half] * 4, "runs", Y_UNIT)
        far = [swap(array, "runs", CORE_UNIT) for array in near]
        return near, far, fitted_own, residual_own, loaded

    def iterate(state):
        turn, pieces, fitted_own = state
        near, far, fitted_own, _, loaded = step(pieces, fitted_own, False)
        (partial,) = call(
            own_half_kernel, "own_half", place, [loaded, *near], [acc], [w_held], flops // 2, in_vmem=(0,)
        )
        pieces = call(
            other_half_kernel, "other_half", place, [loaded, partial, *far], cuts, [w_held, acc_held], flops // 2,
            in_vmem=(0,),
        )
        turn, pieces = lax.optimization_barrier((turn, list(pieces)))
        return turn + 1, pieces, fitted_own

    *pieces, fitted_own = call(
        first_kernel, "first", place, [signs, weights], [*cuts, piece],
        [
            pltpu.VMEM(signs.shape, BF), pltpu.VMEM((blk_dev, k), F32), pltpu.VMEM((blk_dev, k), BF),
            pltpu.SemaphoreType.DMA((5,)),
        ],
        flops, in_hbm=(0, 1),
    )
    _, pieces, fitted_own = lax.while_loop(
        lambda state: state[0] < ITERS - 1, iterate, (jnp.int32(0), pieces, fitted_own)
    )
    near, far, _, residual_own, _ = step(pieces, fitted_own, True)
    held = [pltpu.VMEM((4, width, k), F32), pltpu.SemaphoreType.DMA((4,))]
    whole = [shape((blk_dev, k), F32)]
    fitted = call(functools.partial(place_kernel, 0), "place_near", place, near, whole, held, outs_in_hbm=True)
    (fitted,) = call(
        functools.partial(place_kernel, 1), "place_far", place, [*far, *fitted], whole, held,
        in_hbm=(4,), outs_in_hbm=True, aliases={5: 0},
    )
    return (fitted, residual_own[0])


def solution(mesh):
    in_specs = (P("runs", "blocks"), P("runs", None), P("blocks", None))
    out_specs = (P("blocks", None), P(("runs", "blocks"), None))
    return jax.shard_map(body, mesh=mesh, in_specs=in_specs, out_specs=out_specs, check_vma=False)
```

```python
import functools
import math

import jax
import jax.numpy as jnp
from jax import lax
from jax.experimental import pallas as pl
from jax.experimental.pallas import tpu as pltpu
from jax.sharding import PartitionSpec as P

ITERS = 3
BF = jnp.bfloat16
F32 = jnp.float32

X_UNIT, ZHI_UNIT = 4, 1
Y_UNIT, ZLO_UNIT, CORE_UNIT = 4, 2, 1
AT_X, AT_ZHI, AT_Y, AT_CORE = ("blocks", 2, 3), ("blocks", 0, 3), ("runs", 2, 3), ("runs", 0, 1)


def coordinate(at):
    axis, shift, bits = at
    return (lax.axis_index(axis) >> shift) & bits

VMEM_LIMIT = 16 << 20


def shrink(moved, limit_value):
    size = jnp.maximum(jnp.abs(moved) - limit_value, 0.0)
    return jnp.where(moved < 0.0, -size, size)


def swap(array, axis, flip):
    return lax.ppermute(array, axis, [(i, i ^ flip) for i in range(lax.axis_size(axis))])


def swap4(pieces, axis, unit):
    return [swap(pieces[s], axis, s * unit) for s in (1, 2, 3)]


def call(kernel, name, args, outs, scratch=(), flops=0, in_hbm=(), in_vmem=(), outs_in_hbm=False, aliases=None):
    vmem, hbm = (pl.BlockSpec(memory_space=m) for m in (pltpu.VMEM, pltpu.HBM))
    moved = sum(math.prod(a.shape) * a.dtype.itemsize for a in [*args, *outs])
    args = list(args)
    for i in in_hbm:
        args[i] = pltpu.with_memory_space_constraint(args[i], pltpu.HBM)
    for i in in_vmem:
        args[i] = pltpu.with_memory_space_constraint(args[i], pltpu.VMEM)
    return pl.pallas_call(
        kernel,
        in_specs=[hbm if i in in_hbm else vmem for i in range(len(args))],
        out_specs=[hbm if outs_in_hbm else vmem] * len(outs),
        out_shape=list(outs),
        scratch_shapes=list(scratch),
        input_output_aliases=aliases or {},
        compiler_params=pltpu.CompilerParams(vmem_limit_bytes=VMEM_LIMIT),
        cost_estimate=pl.CostEstimate(flops=flops, bytes_accessed=moved, transcendentals=0),
        name=name,
    )(*args)


def shape(dims, dtype):
    return jax.ShapeDtypeStruct(dims, dtype)


def part(index, size):
    return pl.ds(pl.multiple_of(index * size, size), size)


def cut(acc, outs):
    for s, out in enumerate(outs):
        out[...] = acc[part(coordinate(AT_X) ^ s, out.shape[0]), :].astype(out.dtype)


def first_kernel(s_hbm, w_hbm, p0, p1, p2, p3, own_ref, s_ref, w_held, half, sems):
    rows, width = p0.shape[0], own_ref.shape[1]
    load_w = pltpu.make_async_copy(w_hbm, w_held, sems.at[4])
    load_w.start()
    loads = []
    for s in range(4):
        at = part(coordinate(AT_X) ^ s, rows)
        loads.append(pltpu.make_async_copy(s_hbm.at[at, :], s_ref.at[at, :], sems.at[s]))
        loads[s].start()
    load_w.wait()
    half[...] = w_held[...].astype(BF)
    own_ref[...] = w_held[part(coordinate(AT_CORE) * 4 + coordinate(AT_Y), width), :].T
    for s, out in enumerate((p0, p1, p2, p3)):
        loads[s].wait()
        at = part(coordinate(AT_X) ^ s, rows)
        out[...] = jnp.dot(s_ref[at, :], half[...], preferred_element_type=F32).astype(out.dtype)


def load_kernel(s_hbm, after, s_ref, sems):
    rows = s_ref.shape[0] // 4
    loads = [pltpu.make_async_copy(s_hbm.at[part(i, rows), :], s_ref.at[part(i, rows), :], sems.at[i]) for i in range(4)]
    for load in loads:
        load.start()
    for load in loads:
        load.wait()


def half_product(other, s_ref, pieces, held):
    half = held.shape[1]
    for s, piece in enumerate(pieces):
        held[:, part(coordinate(AT_Y) ^ s, half // 4)] = piece[...]
    columns = part(coordinate(AT_CORE) ^ other, half)
    return lax.dot_general(s_ref[:, columns], held[...], (((1,), (1,)), ((), ())), preferred_element_type=F32)


def own_half_kernel(s_ref, w0, w1, w2, w3, acc_ref, held):
    acc_ref[...] = half_product(0, s_ref, (w0, w1, w2, w3), held)


def other_half_kernel(s_ref, acc_ref, w0, w1, w2, w3, p0, p1, p2, p3, held, acc):
    acc[...] = acc_ref[...] + half_product(1, s_ref, (w0, w1, w2, w3), held)
    cut(acc, (p0, p1, p2, p3))


def sum_kernel(p0, g1, g2, g3, sum_ref, half_ref):
    total = (p0[...] + g1[...].astype(F32)) + (g2[...].astype(F32) + g3[...].astype(F32))
    sum_ref[...] = total
    half_ref[...] = total.astype(BF)


def residual_kernel(scale, q_ref, z1, z2, z3, t_ref, half_ref, *own):
    rows = q_ref.shape[0]
    total = (q_ref[...] + z1[...].astype(F32)) + (z2[...].astype(F32) + z3[...].astype(F32))
    residual = total * scale - t_ref[part(coordinate(AT_X), rows), :]
    half_ref[...] = residual.T.astype(BF)
    if own:
        own_ref, held = own
        held[...] = residual
        own_ref[...] = held[part(coordinate(AT_ZHI), own_ref.shape[0]), :]


def gradient_kernel(other, s_ref, r0, r1, r2, r3, out_ref, held):
    rows, half = r0.shape[1], out_ref.shape[1]
    for s, piece in enumerate((r0, r1, r2, r3)):
        held[:, part(coordinate(AT_X) ^ s, rows)] = piece[...]
    columns = part(coordinate(AT_CORE) ^ other, half)
    out_ref[...] = jnp.dot(held[...], s_ref[:, columns], preferred_element_type=F32).astype(out_ref.dtype)


def join_kernel(kept, got, p0, p1, p2, p3):
    width = p0.shape[1]
    for s, out in enumerate((p0, p1, p2, p3)):
        at = part(coordinate(AT_Y) ^ s, width)
        out[...] = (kept[:, at] + got[:, at].astype(F32)).astype(out.dtype)


def half_kernel(p0, g1, g2, g3, half_ref):
    total = (p0[...] + g1[...].astype(F32)) + (g2[...].astype(F32) + g3[...].astype(F32))
    half_ref[...] = total.astype(BF)


def update_kernel(factor, limit_value, kept, got, fitted_ref, new_ref, half_ref):
    gradient = kept[...].astype(F32) + got[...].astype(F32)
    fitted = shrink(fitted_ref[...] - factor * gradient, limit_value)
    new_ref[...] = fitted
    half_ref[...] = fitted.astype(BF)


def place_kernel(other, *refs):
    out_hbm, held, sems = refs[-3:]
    width = held.shape[1]
    copies = []
    for s, piece in enumerate(refs[:4]):
        held[s] = piece[...].astype(F32).T
        rows = part((coordinate(AT_CORE) ^ other) * 4 + (coordinate(AT_Y) ^ s), width)
        copies.append(pltpu.make_async_copy(held.at[s], out_hbm.at[rows, :], sems.at[s]))
        copies[-1].start()
    for copy in copies:
        copy.wait()


def body(signs, targets, weights):
    run_dev, blk_dev = signs.shape
    k = weights.shape[1]
    total_runs = run_dev * lax.axis_size("runs")
    total_blocks = blk_dev * lax.axis_size("blocks")
    scale_factor = 1.0 / math.sqrt(total_blocks)
    step_size = 1.0 / (1.0 + math.sqrt(total_runs / total_blocks)) ** 2
    limit_value = 0.5 * step_size
    rows, width, share = run_dev // 4, blk_dev // 8, run_dev // lax.axis_size("blocks")
    flops = 2 * run_dev * blk_dev * k
    chunk, chunk_half = shape((rows, k), F32), shape((rows, k), BF)
    piece, piece_half = shape((k, width), F32), shape((k, width), BF)
    cuts = [chunk] + [chunk_half] * 3
    acc, acc_held, w_held = shape((run_dev, k), F32), pltpu.VMEM((run_dev, k), F32), pltpu.VMEM((k, blk_dev // 2), BF)

    def load(after):
        (loaded,) = call(
            load_kernel, "load", [signs, after], [pltpu.VMEM(signs.shape, BF)],
            [pltpu.SemaphoreType.DMA((4,))], in_hbm=(0,),
        )
        return loaded

    def step(pieces, fitted_own, last):
        got = swap4(pieces, "blocks", X_UNIT)
        summed, half = call(sum_kernel, "sum", [pieces[0], *got], [chunk, chunk_half])
        got = swap4([half] * 4, "blocks", ZHI_UNIT)
        loaded = load(half)
        half, *residual_own = call(
            functools.partial(residual_kernel, scale_factor), "residual", [summed, *got, targets],
            [shape((k, rows), BF)] + [shape((share, k), F32)] * last, [pltpu.VMEM((rows, k), F32)] * last,
        )
        halves = [half] + swap4([half] * 4, "blocks", X_UNIT)
        held = [pltpu.VMEM((k, run_dev), BF)]
        (sent,) = call(
            functools.partial(gradient_kernel, 1), "gradient_sent", [loaded, *halves],
            [shape((k, blk_dev // 2), BF)], held, flops // 2, in_vmem=(0,),
        )
        got = swap(sent, "runs", CORE_UNIT)
        (kept,) = call(
            functools.partial(gradient_kernel, 0), "gradient_kept", [loaded, *halves],
            [shape((k, blk_dev // 2), F32)], held, flops // 2, in_vmem=(0,),
        )
        pieces = call(join_kernel, "join", [kept, got], [piece] + [piece_half] * 3)
        got = swap4(pieces, "runs", Y_UNIT)
        (half,) = call(half_kernel, "half", [pieces[0], *got], [piece_half])
        got = swap(half, "runs", ZLO_UNIT)
        fitted_own, half = call(
            functools.partial(update_kernel, step_size * scale_factor, limit_value), "update",
            [half, got, fitted_own], [piece, piece_half], aliases={2: 0},
        )
        near = [half] + swap4([half] * 4, "runs", Y_UNIT)
        far = [swap(array, "runs", CORE_UNIT) for array in near]
        return near, far, fitted_own, residual_own, loaded

    def iterate(state):
        turn, pieces, fitted_own = state
        near, far, fitted_own, _, loaded = step(pieces, fitted_own, False)
        (partial,) = call(
            own_half_kernel, "own_half", [loaded, *near], [acc], [w_held], flops // 2, in_vmem=(0,)
        )
        pieces = call(
            other_half_kernel, "other_half", [loaded, partial, *far], cuts, [w_held, acc_held], flops // 2,
            in_vmem=(0,),
        )
        turn, pieces = lax.optimization_barrier((turn, list(pieces)))
        return turn + 1, pieces, fitted_own

    *pieces, fitted_own = call(
        first_kernel, "first", [signs, weights], [*cuts, piece],
        [
            pltpu.VMEM(signs.shape, BF), pltpu.VMEM((blk_dev, k), F32), pltpu.VMEM((blk_dev, k), BF),
            pltpu.SemaphoreType.DMA((5,)),
        ],
        flops, in_hbm=(0, 1),
    )
    _, pieces, fitted_own = lax.while_loop(
        lambda state: state[0] < ITERS - 1, iterate, (jnp.int32(0), pieces, fitted_own)
    )
    near, far, _, residual_own, _ = step(pieces, fitted_own, True)
    held = [pltpu.VMEM((4, width, k), F32), pltpu.SemaphoreType.DMA((4,))]
    whole = [shape((blk_dev, k), F32)]
    fitted = call(functools.partial(place_kernel, 0), "place_near", near, whole, held, outs_in_hbm=True)
    (fitted,) = call(
        functools.partial(place_kernel, 1), "place_far", [*far, *fitted], whole, held,
        in_hbm=(4,), outs_in_hbm=True, aliases={4: 0},
    )
    return (fitted, residual_own[0])


def solution(mesh):
    in_specs = (P("runs", "blocks"), P("runs", None), P("blocks", None))
    out_specs = (P("blocks", None), P(("runs", "blocks"), None))
    return jax.shard_map(body, mesh=mesh, in_specs=in_specs, out_specs=out_specs, check_vma=False)
```

```python
import functools
import math

import jax
import jax.numpy as jnp
from jax import lax
from jax.experimental import pallas as pl
from jax.experimental.pallas import tpu as pltpu
from jax.sharding import PartitionSpec as P

ITERS = 3
BF = jnp.bfloat16
F32 = jnp.float32

X_UNIT, ZHI_UNIT = 4, 1
Y_UNIT, ZLO_UNIT, CORE_UNIT = 4, 2, 1
AT_X, AT_ZHI, AT_Y, AT_CORE = ("blocks", 2, 3), ("blocks", 0, 3), ("runs", 2, 3), ("runs", 0, 1)


def coordinate(at):
    axis, shift, bits = at
    return (lax.axis_index(axis) >> shift) & bits

VMEM_LIMIT = 16 << 20


def shrink(moved, limit_value):
    size = jnp.maximum(jnp.abs(moved) - limit_value, 0.0)
    return jnp.where(moved < 0.0, -size, size)


def swap(array, axis, flip):
    return lax.ppermute(array, axis, [(i, i ^ flip) for i in range(lax.axis_size(axis))])


def swap4(pieces, axis, unit):
    return [swap(pieces[s], axis, s * unit) for s in (1, 2, 3)]


def call(kernel, name, args, outs, scratch=(), flops=0, in_hbm=(), in_vmem=(), outs_in_hbm=(), aliases=None):
    vmem, hbm = (pl.BlockSpec(memory_space=m) for m in (pltpu.VMEM, pltpu.HBM))
    moved = sum(math.prod(a.shape) * a.dtype.itemsize for a in [*args, *outs])
    args = list(args)
    for i in in_hbm:
        args[i] = pltpu.with_memory_space_constraint(args[i], pltpu.HBM)
    for i in in_vmem:
        args[i] = pltpu.with_memory_space_constraint(args[i], pltpu.VMEM)
    return pl.pallas_call(
        kernel,
        in_specs=[hbm if i in in_hbm else vmem for i in range(len(args))],
        out_specs=[hbm if i in outs_in_hbm else vmem for i in range(len(outs))],
        out_shape=list(outs),
        scratch_shapes=list(scratch),
        input_output_aliases=aliases or {},
        compiler_params=pltpu.CompilerParams(vmem_limit_bytes=VMEM_LIMIT),
        cost_estimate=pl.CostEstimate(flops=flops, bytes_accessed=moved, transcendentals=0),
        name=name,
    )(*args)


def shape(dims, dtype):
    return jax.ShapeDtypeStruct(dims, dtype)


def part(index, size):
    return pl.ds(pl.multiple_of(index * size, size), size)


def cut(acc, outs):
    for s, out in enumerate(outs):
        out[...] = acc[part(coordinate(AT_X) ^ s, out.shape[0]), :].astype(out.dtype)


def first_kernel(s_hbm, w_hbm, p0, p1, p2, p3, own_ref, s_ref, w_held, half, sems):
    rows, width = p0.shape[0], own_ref.shape[1]
    load_w = pltpu.make_async_copy(w_hbm, w_held, sems.at[4])
    load_w.start()
    loads = []
    for s in range(4):
        at = part(coordinate(AT_X) ^ s, rows)
        loads.append(pltpu.make_async_copy(s_hbm.at[at, :], s_ref.at[at, :], sems.at[s]))
        loads[s].start()
    load_w.wait()
    half[...] = w_held[...].astype(BF)
    own_ref[...] = w_held[part(coordinate(AT_CORE) * 4 + coordinate(AT_Y), width), :].T
    for s, out in enumerate((p0, p1, p2, p3)):
        loads[s].wait()
        at = part(coordinate(AT_X) ^ s, rows)
        out[...] = jnp.dot(s_ref[at, :], half[...], preferred_element_type=F32).astype(out.dtype)


def load_kernel(s_hbm, after, s_ref, sems):
    rows = s_ref.shape[0] // 4
    loads = [pltpu.make_async_copy(s_hbm.at[part(i, rows), :], s_ref.at[part(i, rows), :], sems.at[i]) for i in range(4)]
    for load in loads:
        load.start()
    for load in loads:
        load.wait()


def load_and_store_kernel(s_hbm, residual_ref, s_ref, own_hbm, sems, store_sem):
    rows = part(coordinate(AT_ZHI), own_hbm.shape[0])
    store = pltpu.make_async_copy(residual_ref.at[rows, :], own_hbm, store_sem)
    store.start()
    load_kernel(s_hbm, residual_ref, s_ref, sems)
    store.wait()


def half_product(other, s_ref, pieces, held):
    half = held.shape[1]
    for s, piece in enumerate(pieces):
        held[:, part(coordinate(AT_Y) ^ s, half // 4)] = piece[...]
    columns = part(coordinate(AT_CORE) ^ other, half)
    return lax.dot_general(s_ref[:, columns], held[...], (((1,), (1,)), ((), ())), preferred_element_type=F32)


def own_half_kernel(s_ref, w0, w1, w2, w3, acc_ref, held):
    acc_ref[...] = half_product(0, s_ref, (w0, w1, w2, w3), held)


def other_half_kernel(s_ref, acc_ref, w0, w1, w2, w3, p0, p1, p2, p3, held, acc):
    acc[...] = acc_ref[...] + half_product(1, s_ref, (w0, w1, w2, w3), held)
    cut(acc, (p0, p1, p2, p3))


def sum_kernel(p0, g1, g2, g3, sum_ref, half_ref):
    total = (p0[...] + g1[...].astype(F32)) + (g2[...].astype(F32) + g3[...].astype(F32))
    sum_ref[...] = total
    half_ref[...] = total.astype(BF)


def residual_kernel(scale, q_ref, z1, z2, z3, t_ref, half_ref, *whole):
    total = (q_ref[...] + z1[...].astype(F32)) + (z2[...].astype(F32) + z3[...].astype(F32))
    residual = total * scale - t_ref[part(coordinate(AT_X), q_ref.shape[0]), :]
    half_ref[...] = residual.T.astype(BF)
    for out in whole:
        out[...] = residual


def gradient_kernel(other, s_ref, r0, r1, r2, r3, out_ref, held):
    rows, half = r0.shape[1], out_ref.shape[1]
    for s, piece in enumerate((r0, r1, r2, r3)):
        held[:, part(coordinate(AT_X) ^ s, rows)] = piece[...]
    columns = part(coordinate(AT_CORE) ^ other, half)
    out_ref[...] = jnp.dot(held[...], s_ref[:, columns], preferred_element_type=F32).astype(out_ref.dtype)


def join_kernel(kept, got, p0, p1, p2, p3):
    width = p0.shape[1]
    for s, out in enumerate((p0, p1, p2, p3)):
        at = part(coordinate(AT_Y) ^ s, width)
        out[...] = (kept[:, at] + got[:, at].astype(F32)).astype(out.dtype)


def half_kernel(p0, g1, g2, g3, half_ref):
    total = (p0[...] + g1[...].astype(F32)) + (g2[...].astype(F32) + g3[...].astype(F32))
    half_ref[...] = total.astype(BF)


def update_kernel(factor, limit_value, kept, got, fitted_ref, new_ref, half_ref):
    gradient = kept[...].astype(F32) + got[...].astype(F32)
    fitted = shrink(fitted_ref[...] - factor * gradient, limit_value)
    new_ref[...] = fitted
    half_ref[...] = fitted.astype(BF)


def place_kernel(other, *refs):
    out_hbm, held, sems = refs[-3:]
    width = held.shape[1]
    copies = []
    for s, piece in enumerate(refs[:4]):
        held[s] = piece[...].astype(F32).T
        rows = part((coordinate(AT_CORE) ^ other) * 4 + (coordinate(AT_Y) ^ s), width)
        copies.append(pltpu.make_async_copy(held.at[s], out_hbm.at[rows, :], sems.at[s]))
        copies[-1].start()
    for copy in copies:
        copy.wait()


def body(signs, targets, weights):
    run_dev, blk_dev = signs.shape
    k = weights.shape[1]
    total_runs = run_dev * lax.axis_size("runs")
    total_blocks = blk_dev * lax.axis_size("blocks")
    scale_factor = 1.0 / math.sqrt(total_blocks)
    step_size = 1.0 / (1.0 + math.sqrt(total_runs / total_blocks)) ** 2
    limit_value = 0.5 * step_size
    rows, width, share = run_dev // 4, blk_dev // 8, run_dev // lax.axis_size("blocks")
    flops = 2 * run_dev * blk_dev * k
    chunk, chunk_half = shape((rows, k), F32), shape((rows, k), BF)
    piece, piece_half = shape((k, width), F32), shape((k, width), BF)
    cuts = [chunk] + [chunk_half] * 3
    acc, acc_held, w_held = shape((run_dev, k), F32), pltpu.VMEM((run_dev, k), F32), pltpu.VMEM((k, blk_dev // 2), BF)

    def load(after):
        (loaded,) = call(
            load_kernel, "load", [signs, after], [pltpu.VMEM(signs.shape, BF)],
            [pltpu.SemaphoreType.DMA((4,))], in_hbm=(0,),
        )
        return loaded

    def step(pieces, fitted_own, last):
        got = swap4(pieces, "blocks", X_UNIT)
        summed, half = call(sum_kernel, "sum", [pieces[0], *got], [chunk, chunk_half])
        got = swap4([half] * 4, "blocks", ZHI_UNIT)
        after = half
        half, *residual = call(
            functools.partial(residual_kernel, scale_factor), "residual", [summed, *got, targets],
            [shape((k, rows), BF)] + [pltpu.VMEM((rows, k), F32)] * last,
        )
        residual_own = None
        if last:
            loaded, residual_own = call(
                load_and_store_kernel, "load", [signs, *residual], [pltpu.VMEM(signs.shape, BF), shape((share, k), F32)],
                [pltpu.SemaphoreType.DMA((4,)), pltpu.SemaphoreType.DMA], in_hbm=(0,), in_vmem=(1,), outs_in_hbm=(1,),
            )
        else:
            loaded = load(after)
        halves = [half] + swap4([half] * 4, "blocks", X_UNIT)
        held = [pltpu.VMEM((k, run_dev), BF)]
        (sent,) = call(
            functools.partial(gradient_kernel, 1), "gradient_sent", [loaded, *halves],
            [shape((k, blk_dev // 2), BF)], held, flops // 2, in_vmem=(0,),
        )
        got = swap(sent, "runs", CORE_UNIT)
        (kept,) = call(
            functools.partial(gradient_kernel, 0), "gradient_kept", [loaded, *halves],
            [shape((k, blk_dev // 2), F32)], held, flops // 2, in_vmem=(0,),
        )
        pieces = call(join_kernel, "join", [kept, got], [piece] + [piece_half] * 3)
        got = swap4(pieces, "runs", Y_UNIT)
        (half,) = call(half_kernel, "half", [pieces[0], *got], [piece_half])
        got = swap(half, "runs", ZLO_UNIT)
        fitted_own, half = call(
            functools.partial(update_kernel, step_size * scale_factor, limit_value), "update",
            [half, got, fitted_own], [piece, piece_half], aliases={2: 0},
        )
        near = [half] + swap4([half] * 4, "runs", Y_UNIT)
        far = [swap(array, "runs", CORE_UNIT) for array in near]
        return near, far, fitted_own, residual_own, loaded

    def iterate(state):
        turn, pieces, fitted_own = state
        near, far, fitted_own, _, loaded = step(pieces, fitted_own, False)
        (partial,) = call(
            own_half_kernel, "own_half", [loaded, *near], [acc], [w_held], flops // 2, in_vmem=(0,)
        )
        pieces = call(
            other_half_kernel, "other_half", [loaded, partial, *far], cuts, [w_held, acc_held], flops // 2,
            in_vmem=(0,),
        )
        turn, pieces = lax.optimization_barrier((turn, list(pieces)))
        return turn + 1, pieces, fitted_own

    *pieces, fitted_own = call(
        first_kernel, "first", [signs, weights], [*cuts, piece],
        [
            pltpu.VMEM(signs.shape, BF), pltpu.VMEM((blk_dev, k), F32), pltpu.VMEM((blk_dev, k), BF),
            pltpu.SemaphoreType.DMA((5,)),
        ],
        flops, in_hbm=(0, 1),
    )
    _, pieces, fitted_own = lax.while_loop(
        lambda state: state[0] < ITERS - 1, iterate, (jnp.int32(0), pieces, fitted_own)
    )
    near, far, _, residual_own, _ = step(pieces, fitted_own, True)
    held = [pltpu.VMEM((4, width, k), F32), pltpu.SemaphoreType.DMA((4,))]
    whole = [shape((blk_dev, k), F32)]
    fitted = call(functools.partial(place_kernel, 0), "place_near", near, whole, held, outs_in_hbm=(0,))
    (fitted,) = call(
        functools.partial(place_kernel, 1), "place_far", [*far, *fitted], whole, held,
        in_hbm=(4,), outs_in_hbm=(0,), aliases={4: 0},
    )
    return (fitted, residual_own)


def solution(mesh):
    in_specs = (P("runs", "blocks"), P("runs", None), P("blocks", None))
    out_specs = (P("blocks", None), P(("runs", "blocks"), None))
    return jax.shard_map(body, mesh=mesh, in_specs=in_specs, out_specs=out_specs, check_vma=False)
```
